256 devices in a mesh: outer: 64 (over x, y_hi, z), inner: 4 (over y_lo, core).
Axes of the slice: x: 4, y: 4 (y_hi: 2, y_lo: 2; y = y_hi * 2 + y_lo), z: 8, core: 2. Of those that a mesh axis runs over, the one named last changes fastest.
Arguments:
- query_rows: bfloat16 [65536, 1024], P(('outer', 'inner')), may hold values from -8 to 8
- key_rows: bfloat16 [65536, 128], P(('outer', 'inner')), may hold values from -4 to 4
- value_rows: bfloat16 [65536, 128], P(('outer', 'inner')), may hold values from -6 to 6
- out_grad: bfloat16 [65536, 1024], P(('outer', 'inner')), may hold values from -6 to 6
- piece_ids: int32 [512], replicated, may hold values from 0 to 511, as said below
- key_pieces: int32 [512, 16], P('outer'), may hold values from -1 to 511, as said below
Outputs:
- query_grad: bfloat16 [65536, 1024], P(('outer', 'inner'))
- key_grad: bfloat16 [65536, 128], P(('outer', 'inner'))
- value_grad: bfloat16 [65536, 128], P(('outer', 'inner'))
The draws below stay inside these ranges and needn't reach their ends.
Inputs may be any that keep to these rules, and one draw needn't show every extreme that they name: `piece_ids`: each piece once. Piece p is the one of tokens p * 128 to (p + 1) * 128 - 1 of the sequence. The slots g * 2 * 4 to (g + 1) * 2 * 4 - 1 hold, in some order, the pieces g * 4 to (g + 1) * 4 - 1 and (127 - g) * 4 to (128 - g) * 4 - 1. `key_pieces`: -1 marks an empty entry, in any position. Row s names its own piece piece_ids[s], no piece twice, only pieces no later than its own, and only pieces held by slots of the same group as s or of the group below it (group 0 with group 64 - 1), the group of slot s being s // 8.
All inputs are finite; a program needn't handle non-finite values.
Results may differ from the reference program's by a relative error of at most 0.04.
Values may be sent and summed in bfloat16 or wider, within the bound.
A program may use at most 64 MiB of HBM per device.

```python
import jax
import jax.numpy as jnp
from jax import lax

H = 8
HD = 128
PIECE = 128
PIECES = 512
TOKENS = 65536
GROUPS = 64
BLOCK_PIECES = 4
LISTED = 16


def layout(key):
    group_index = jnp.arange(GROUPS, dtype=jnp.int32)[:, None]
    position = jnp.arange(2 * BLOCK_PIECES, dtype=jnp.int32)[None, :]
    first_half = group_index * BLOCK_PIECES + position
    second = (2 * GROUPS - 1 - group_index) * BLOCK_PIECES + position - BLOCK_PIECES
    ordered = jnp.where(position < BLOCK_PIECES, first_half, second)
    orders = jax.vmap(lambda subkey: jax.random.permutation(subkey, 2 * BLOCK_PIECES))(jax.random.split(key, GROUPS))
    return jnp.take_along_axis(ordered, orders.astype(jnp.int32), axis=1).astype(jnp.int32)


def draw_piece_ids(key, part):
    placed = layout(key)
    return placed.reshape(PIECES).astype(jnp.int32)


def draw_key_pieces(key, part):
    placed = layout(key)
    key = jax.random.fold_in(key, 5)
    below = jnp.roll(placed, 1, axis=0)
    candidates = jnp.concatenate([placed, below], axis=1)
    mine = placed[:, :, None]
    offered = jnp.broadcast_to(candidates[:, None, :], (GROUPS, 2 * BLOCK_PIECES, 4 * BLOCK_PIECES))
    chosen = jax.random.randint(key, offered.shape, 0, 2) == 1
    listed = (offered == mine) | (offered < mine) & chosen
    entries = jnp.where(listed, offered, -1).reshape(PIECES, LISTED)
    shuffle = jax.vmap(lambda subkey: jax.random.permutation(subkey, LISTED))(jax.random.split(jax.random.fold_in(key, 9), PIECES))
    return jnp.take_along_axis(entries, shuffle.astype(jnp.int32), axis=1).astype(jnp.int32)


def draw_query_rows(key, part):
    key = jax.random.fold_in(key, 1)
    drawn = jnp.clip(jax.random.normal(key, (TOKENS, H, HD), jnp.float32), -6.0, 6.0)
    return drawn.reshape(TOKENS, H * HD).astype(jnp.bfloat16)


def draw_key_rows(key, part):
    key = jax.random.fold_in(key, 2)
    drawn = jnp.clip(jax.random.normal(key, (TOKENS, HD), jnp.float32), -4.0, 4.0)
    return drawn.astype(jnp.bfloat16)


def level_of(key, shape, shards, low, high):
    factor_of = 1.0
    for dim, parts in shards:
        steps = jax.random.uniform(jax.random.fold_in(jax.random.fold_in(key, 6), dim), (parts,), jnp.float32, low / len(shards), high / len(shards))
        factor_of = factor_of * jnp.repeat(jnp.exp(steps), shape[dim] // parts).reshape((-1,) + (1,) * (len(shape) - 1 - dim))
    return factor_of


def normal_values(own_key, extent, spread, bound, shards=(), held_as=jnp.bfloat16):
    array = spread * jax.random.normal(own_key, extent, jnp.float32)
    if shards:
        array = array * level_of(own_key, extent, shards, -0.22, 0.18)
    return jnp.clip(array, -bound, bound).astype(held_as)


def setup_inputs(seed: int = 0) -> dict:
    keys = jax.random.split(jax.random.key(seed), 7)
    return {
        "query_rows": draw_query_rows(jax.random.fold_in(keys[6], 71), 0),
        "key_rows": draw_key_rows(jax.random.fold_in(keys[6], 71), 0),
        "value_rows": normal_values(keys[2], (TOKENS, HD), 1.0, 6.0, ((0, 256),)),
        "out_grad": normal_values(keys[3], (TOKENS, H * HD), 1.0, 6.0, ((0, 256),)),
        "piece_ids": draw_piece_ids(jax.random.fold_in(keys[6], 71), 0),
        "key_pieces": draw_key_pieces(jax.random.fold_in(keys[6], 71), 0),
    }


def reference(query_rows, key_rows, value_rows, out_grad, piece_ids, key_pieces):
    scaling = HD ** -0.5
    slot_index = jnp.arange(PIECES, dtype=jnp.int32)
    inverse = jnp.zeros((PIECES,), jnp.int32).at[piece_ids].set(slot_index)
    query_pieces = query_rows.reshape(PIECES, PIECE, H, HD)
    key_slots = key_rows.reshape(PIECES, PIECE, HD)
    value_slots = value_rows.reshape(PIECES, PIECE, HD)
    grad_pieces = out_grad.reshape(PIECES, PIECE, H, HD)
    offsets = jnp.arange(PIECE, dtype=jnp.int32)
    causal = offsets[None, None, :] <= offsets[:, None, None]

    def per_slot(accumulated, slot_now):
        listing = key_pieces[slot_now]
        present = listing >= 0
        source = inverse[jnp.maximum(listing, 0)].astype(jnp.int32)
        same_piece = listing == piece_ids[slot_now]
        allowed = (present[None, :, None] & (jnp.logical_not(same_piece)[None, :, None] | causal)).reshape(PIECE, LISTED * PIECE)
        queries = query_pieces[slot_now].astype(jnp.float32)
        grad_here = grad_pieces[slot_now].astype(jnp.float32)
        keys_here = key_slots[source].reshape(LISTED * PIECE, HD).astype(jnp.float32)
        values_here = value_slots[source].reshape(LISTED * PIECE, HD).astype(jnp.float32)
        scores = jnp.einsum("qhd,kd->hqk", queries, keys_here) * scaling
        largest = jnp.max(jnp.where(allowed[None], scores, -jnp.inf), axis=2)
        log_norm = largest + jnp.log(jnp.sum(jnp.where(allowed[None], jnp.exp(scores - largest[:, :, None]), 0.0), axis=2))
        weights = jnp.where(allowed[None], jnp.exp(scores - log_norm[:, :, None]), 0.0)
        weights_low = lax.optimization_barrier(weights.astype(jnp.bfloat16)).astype(jnp.float32)
        attended = jnp.einsum("hqk,kd->qhd", weights_low, values_here)
        attended = lax.optimization_barrier(attended.astype(jnp.bfloat16)).astype(jnp.float32)
        row_delta = jnp.sum(grad_here * attended, axis=2).T
        dweights = jnp.einsum("qhd,kd->hqk", grad_here, values_here)
        dscores = lax.optimization_barrier((weights * (dweights - row_delta[:, :, None])).astype(jnp.bfloat16)).astype(jnp.float32)
        query_term = jnp.einsum("hqk,kd->qhd", dscores, keys_here) * scaling
        key_term = jnp.einsum("hqk,qhd->kd", dscores, queries) * scaling
        value_term = jnp.einsum("hqk,qhd->kd", weights_low, grad_here)
        update = jnp.stack([key_term, value_term], axis=1).reshape(LISTED, PIECE, 2, HD)
        accumulated = accumulated.at[source].add(update)
        return accumulated, query_term.astype(jnp.bfloat16)

    initial = jnp.zeros((PIECES, PIECE, 2, HD), jnp.float32)
    accumulated, query_terms = lax.scan(per_slot, initial, slot_index)
    query_grad = query_terms.reshape(TOKENS, H * HD)
    key_grad = accumulated[:, :, 0].reshape(TOKENS, HD).astype(jnp.bfloat16)
    value_grad = accumulated[:, :, 1].reshape(TOKENS, HD).astype(jnp.bfloat16)
    return (query_grad, key_grad, value_grad)
```

```python
import functools

import jax
import jax.numpy as jnp
from jax import lax
from jax.experimental import pallas as pl
from jax.experimental.pallas import tpu as pltpu
from jax.sharding import PartitionSpec as P

MESH = pl.DeviceIdType.MESH
F32 = jnp.float32
BF16 = jnp.bfloat16
LOG2E = 1.4426950408889634
FILL = -1e30


def dot_nt(a, b):
    return lax.dot_general(a, b, (((1,), (1,)), ((), ())), preferred_element_type=F32)


def dot_nn(a, b):
    return lax.dot_general(a, b, (((1,), (0,)), ((), ())), preferred_element_type=F32)


def kernel(
    outer_count,
    heads,
    q_ref,
    g_ref,
    k_ref,
    v_ref,
    ids_hbm,
    lists_hbm,
    dq_ref,
    dk_ref,
    dv_ref,
    kv,
    qg,
    qgt,
    kt,
    prob,
    dprob,
    top,
    total,
    dtotal,
    bias,
    stat,
    factor,
    delta,
    term,
    term_in,
    own_term,
    dq_out,
    dq_in,
    ids_ref,
    lists_ref,
    load_sem,
    kv_send,
    kv_recv,
    qg_send,
    qg_recv,
    stat_sem,
    term_send,
    term_recv,
    dq_sem,
):
    rows = k_ref.shape[0]
    width = k_ref.shape[1]
    piece = rows // 2
    tiles = 2 * heads
    half = heads * rows
    scale = width**-0.5
    scale2 = scale * LOG2E

    outer = lax.axis_index("outer")
    inner = lax.axis_index("inner")
    core = lax.rem(inner, 2)
    other = inner + 1 - 2 * core
    across = lax.rem(inner + 2, 4)
    up = lax.rem(outer + 1, outer_count)
    down = lax.rem(outer + outer_count - 1, outer_count)
    sibling = (outer, other)
    beside = (outer, across)

    def remote(src, dst, send, recv, device):
        return pltpu.make_async_remote_copy(
            src_ref=src, dst_ref=dst, send_sem=send, recv_sem=recv, device_id=device, device_id_type=MESH
        )

    loads_ids = [
        pltpu.make_async_copy(ids_hbm, ids_ref, load_sem.at[4]),
        pltpu.make_async_copy(lists_hbm, lists_ref, load_sem.at[5]),
    ]
    for c in loads_ids:
        c.start()
    loads_kv = [
        pltpu.make_async_copy(k_ref, kv.at[0, 0], load_sem.at[0]),
        pltpu.make_async_copy(v_ref, kv.at[1, 0], load_sem.at[1]),
    ]
    for c in loads_kv:
        c.start()
    loads_q = []
    for which, src in ((0, q_ref), (1, g_ref)):
        for h in range(heads):
            loads_q.append(
                pltpu.make_async_copy(
                    src.at[:, pl.ds(h * width, width)],
                    qg.at[which, pl.ds(h * rows, rows)],
                    load_sem.at[2 + which],
                )
            )
    for c in loads_q:
        c.start()

    barrier = pltpu.get_barrier_semaphore()
    for device in (sibling, beside, (up, inner), (down, inner), (up, across), (down, across)):
        pl.semaphore_signal(barrier, inc=1, device_id=device, device_id_type=MESH)
    pl.semaphore_wait(barrier, 6)

    kv_sends = []
    for slot, device in ((2, (up, inner)), (3, (up, across)), (1, beside)):
        for which, src in ((0, k_ref), (1, v_ref)):
            index = 2 * slot + which
            c = remote(src, kv.at[which, slot], kv_send.at[index], kv_recv.at[index], device)
            c.start()
            kv_sends.append((index, c))
    by_index = dict(kv_sends)
    for which, src in ((0, q_ref), (1, g_ref)):
        for h in range(heads):
            c = remote(
                src.at[:, pl.ds(h * width, width)],
                qg.at[which, pl.ds(half + h * rows, rows)],
                qg_send.at[which],
                qg_recv.at[which],
                sibling,
            )
            c.start()

    for c in loads_ids:
        c.wait()
    slot_index = lax.broadcasted_iota(jnp.int32, (8, 1), 0)
    ids = jnp.zeros((8, 1), jnp.int32)
    for slot, (group, device) in enumerate(
        ((outer, inner), (outer, across), (down, inner), (down, across))
    ):
        for a in range(2):
            ids = jnp.where(slot_index == 2 * slot + a, ids_ref[group * 8 + device * 2 + a], ids)
    for who, device in ((0, inner), (1, other)):
        parts = []
        for a in range(2):
            row = lists_ref[pl.ds(2 * device + a, 1), :]
            hit = jnp.max(jnp.where(row == ids, 1.0, 0.0), axis=1, keepdims=True)
            parts.append(jnp.broadcast_to((hit - 1.0) * (-FILL), (8, piece)))
        both = jnp.concatenate(parts, axis=1)
        for j in range(8):
            bias[who, j] = jnp.broadcast_to(both[j : j + 1], (8, rows))

    causal = lax.broadcasted_iota(jnp.int32, (piece, piece), 0) <= lax.broadcasted_iota(
        jnp.int32, (piece, piece), 1
    )

    def scores(slot, who):
        def head(h, _):
            t = who * heads + h
            lanes = pl.ds(pl.multiple_of(t * rows, rows), rows)
            s = dot_nt(kv[0, slot], qg[0, lanes, :])
            g = dot_nt(kv[1, slot], qg[1, lanes, :])
            for a in range(2):
                sa = s[a * piece : (a + 1) * piece]
                ga = g[a * piece : (a + 1) * piece]
                if slot == 0 and who == 0:
                    cut = jnp.where(causal, sa[:, a * piece : (a + 1) * piece], FILL)
                    sa = jnp.concatenate(
                        [cut, sa[:, piece:]] if a == 0 else [sa[:, :piece], cut], axis=1
                    )
                s3 = sa.reshape(piece // 8, 8, rows)
                g3 = ga.reshape(piece // 8, 8, rows)
                m = jnp.max(s3, axis=0)
                p = jnp.exp2((s3 - m[None]) * scale2)
                place = pl.ds(slot * rows + a * piece, piece)
                prob[place, lanes] = p.reshape(piece, rows).astype(BF16)
                dprob[place, lanes] = ga.astype(BF16)
                top[t, 2 * slot + a] = m * scale2
                total[t, 2 * slot + a] = jnp.sum(p, axis=0)
                dtotal[t, 2 * slot + a] = jnp.sum(p * g3, axis=0)
            return 0

        lax.fori_loop(0, heads, head, 0, unroll=True)

    def transposed(who):
        def head(h, _):
            lanes = pl.ds(pl.multiple_of((who * heads + h) * rows, rows), rows)
            qgt[0, :, lanes] = qg[0, lanes, :].T
            qgt[1, :, lanes] = qg[1, lanes, :].T
            return 0

        lax.fori_loop(0, heads, head, 0, unroll=True)

    def transposed_keys(slot):
        kt[:, pl.ds(slot * rows, rows)] = kv[0, slot].T

    for c in loads_kv:
        c.wait()
    for which in range(2):
        pltpu.make_async_copy(
            qg.at[which, pl.ds(half, half)], qg.at[which, pl.ds(0, half)], load_sem.at[2 + which]
        ).wait()
    scores(0, 0)
    transposed(0)
    transposed_keys(0)
    qg_all = [
        remote(
            qg.at[which, pl.ds(0, half)],
            qg.at[which, pl.ds(half, half)],
            qg_send.at[which],
            qg_recv.at[which],
            sibling,
        )
        for which in range(2)
    ]
    for c in qg_all:
        c.wait_recv()
    scores(0, 1)
    transposed(1)
    for slot in (1, 2, 3):
        for which in range(2):
            by_index[2 * slot + which].wait_recv()
        scores(slot, 0)
        scores(slot, 1)
        transposed_keys(slot)

    for who in range(2):

        def local(h, _, who=who):
            t = who * heads + h
            mj = top[t] + bias[who]
            m = jnp.max(jnp.max(mj, axis=0), axis=0, keepdims=True)
            w = jnp.exp2(mj - m[None])
            top[t] = w
            stat[0, 0, pl.ds(t, 1)] = m
            stat[0, 1, pl.ds(t, 1)] = jnp.sum(jnp.sum(w * total[t], axis=0), axis=0, keepdims=True)
            stat[0, 2, pl.ds(t, 1)] = jnp.sum(jnp.sum(w * dtotal[t], axis=0), axis=0, keepdims=True)
            return 0

        lax.fori_loop(0, heads, local, 0, unroll=True)
    stat_copy = remote(stat.at[0], stat.at[1], stat_sem.at[0], stat_sem.at[1], sibling)
    stat_copy.start()
    stat_copy.wait()
    mine = [stat[0, c] for c in range(3)]
    theirs = [jnp.concatenate([stat[1, c, heads:], stat[1, c, :heads]], axis=0) for c in range(3)]
    m = jnp.maximum(mine[0], theirs[0])
    e_mine = jnp.exp2(mine[0] - m)
    e_theirs = jnp.exp2(theirs[0] - m)
    inverse = 1.0 / (mine[1] * e_mine + theirs[1] * e_theirs)
    factor[...] = e_mine * inverse
    d = (mine[2] * e_mine + theirs[2] * e_theirs) * inverse
    for t in range(tiles):
        delta[:, pl.ds(t * rows, rows)] = jnp.broadcast_to(d[t : t + 1], (16, rows)).astype(BF16)

    def gradients(slot):
        def tile(t, _):
            lanes = pl.ds(pl.multiple_of(t * rows, rows), rows)
            f = factor[pl.ds(t, 1)]
            de = delta[:, lanes]
            for a in range(2):
                r = (top[t, 2 * slot + a] * f).astype(BF16)
                r = jnp.concatenate([r, r], axis=0)
                place = pl.ds(slot * rows + a * piece, piece)
                p = prob[place, lanes].reshape(piece // 16, 16, rows) * r[None]
                ds = p * (dprob[place, lanes].reshape(piece // 16, 16, rows) - de[None])
                prob[place, lanes] = p.reshape(piece, rows)
                dprob[place, lanes] = ds.reshape(piece, rows)
            return 0

        lax.fori_loop(0, tiles, tile, 0, unroll=True)
        place = pl.ds(slot * rows, rows)
        key_term = dot_nt(qgt[0], dprob[place, :]).T * scale
        value_term = dot_nt(qgt[1], prob[place, :]).T
        return key_term, value_term

    term_copies = []
    for slot, device in ((1, beside), (3, (down, across)), (2, (down, inner))):
        key_term, value_term = gradients(slot)
        term[slot - 1, 0] = key_term.astype(BF16)
        term[slot - 1, 1] = value_term.astype(BF16)
        c = remote(
            term.at[slot - 1],
            term_in.at[slot - 1],
            term_send.at[slot - 1],
            term_recv.at[slot - 1],
            device,
        )
        c.start()
        term_copies.append(c)
    key_term, value_term = gradients(0)
    own_term[0] = key_term
    own_term[1] = value_term

    def query_gradient(t):
        lanes = pl.ds(pl.multiple_of(t * rows, rows), rows)
        return dot_nn(kt[...], dprob[:, lanes]).T * scale

    def theirs_step(h, _):
        dq_out[:, pl.ds(pl.multiple_of(h * width, width), width)] = query_gradient(heads + h).astype(BF16)
        return 0

    lax.fori_loop(0, heads, theirs_step, 0, unroll=True)
    dq_copy = remote(dq_out, dq_in, dq_sem.at[0], dq_sem.at[1], sibling)
    dq_copy.start()
    dq_own = [query_gradient(h) for h in range(heads)]
    dq_copy.wait()
    for h in range(heads):
        lanes = pl.ds(h * width, width)
        dq_ref[:, lanes] = (dq_own[h] + dq_in[:, lanes].astype(F32)).astype(BF16)

    for c in term_copies:
        c.wait()
    dk_ref[...] = (
        own_term[0] + (term_in[0, 0].astype(F32) + term_in[1, 0].astype(F32) + term_in[2, 0].astype(F32))
    ).astype(BF16)
    dv_ref[...] = (
        own_term[1] + (term_in[0, 1].astype(F32) + term_in[1, 1].astype(F32) + term_in[2, 1].astype(F32))
    ).astype(BF16)
    for _, c in kv_sends:
        c.wait_send()
    for c in qg_all:
        c.wait_send()


def solution(mesh):
    outer_count = mesh.shape["outer"]

    def per_device(query_rows, key_rows, value_rows, out_grad, piece_ids, key_pieces):
        rows, width = key_rows.shape
        heads = query_rows.shape[1] // width
        tiles = 2 * heads
        lanes = tiles * rows
        vmem = pl.BlockSpec(memory_space=pltpu.VMEM)
        return pl.pallas_call(
            functools.partial(kernel, outer_count, heads),
            out_shape=[
                jax.ShapeDtypeStruct(query_rows.shape, BF16),
                jax.ShapeDtypeStruct(key_rows.shape, BF16),
                jax.ShapeDtypeStruct(key_rows.shape, BF16),
            ],
            in_specs=[pl.BlockSpec(memory_space=pltpu.HBM)] * 6,
            out_specs=[vmem] * 3,
            scratch_shapes=[
                pltpu.VMEM((2, 4, rows, width), BF16),
                pltpu.VMEM((2, lanes, width), BF16),
                pltpu.VMEM((2, width, lanes), BF16),
                pltpu.VMEM((width, 4 * rows), BF16),
                pltpu.VMEM((4 * rows, lanes), BF16),
                pltpu.VMEM((4 * rows, lanes), BF16),
                pltpu.VMEM((tiles, 8, 8, rows), F32),
                pltpu.VMEM((tiles, 8, 8, rows), F32),
                pltpu.VMEM((tiles, 8, 8, rows), F32),
                pltpu.VMEM((2, 8, 8, rows), F32),
                pltpu.VMEM((2, 3, tiles, rows), F32),
                pltpu.VMEM((tiles, rows), F32),
                pltpu.VMEM((16, lanes), BF16),
                pltpu.VMEM((3, 2, rows, width), BF16),
                pltpu.VMEM((3, 2, rows, width), BF16),
                pltpu.VMEM((2, rows, width), F32),
                pltpu.VMEM(query_rows.shape, BF16),
                pltpu.VMEM(query_rows.shape, BF16),
                pltpu.SMEM(piece_ids.shape, jnp.int32),
                pltpu.VMEM(key_pieces.shape, jnp.int32),
                pltpu.SemaphoreType.DMA((6,)),
                pltpu.SemaphoreType.DMA((8,)),
                pltpu.SemaphoreType.DMA((8,)),
                pltpu.SemaphoreType.DMA((2,)),
                pltpu.SemaphoreType.DMA((2,)),
                pltpu.SemaphoreType.DMA((2,)),
                pltpu.SemaphoreType.DMA((3,)),
                pltpu.SemaphoreType.DMA((3,)),
                pltpu.SemaphoreType.DMA((2,)),
            ],
            compiler_params=pltpu.CompilerParams(
                collective_id=0, has_side_effects=True, vmem_limit_bytes=64 * 1024 * 1024
            ),
            name="attention_backward",
        )(query_rows, out_grad, key_rows, value_rows, piece_ids, key_pieces)

    return jax.shard_map(
        per_device,
        mesh=mesh,
        in_specs=(
            P(("outer", "inner"), None),
            P(("outer", "inner"), None),
            P(("outer", "inner"), None),
            P(("outer", "inner"), None),
            P(),
            P("outer", None),
        ),
        out_specs=(
            P(("outer", "inner"), None),
            P(("outer", "inner"), None),
            P(("outer", "inner"), None),
        ),
        check_vma=False,
    )
```

```python
import functools

import jax
import jax.numpy as jnp
from jax import lax
from jax.experimental import pallas as pl
from jax.experimental.pallas import tpu as pltpu
from jax.sharding import PartitionSpec as P

MESH = pl.DeviceIdType.MESH
F32 = jnp.float32
BF16 = jnp.bfloat16
LOG2E = 1.4426950408889634
FILL = -1e30


def dot_nt(a, b):
    return lax.dot_general(a, b, (((1,), (1,)), ((), ())), preferred_element_type=F32)


def dot_nn(a, b):
    return lax.dot_general(a, b, (((1,), (0,)), ((), ())), preferred_element_type=F32)


def kernel(
    outer_count,
    heads,
    q_ref,
    g_ref,
    k_ref,
    v_ref,
    ids_hbm,
    lists_hbm,
    dq_ref,
    dk_ref,
    dv_ref,
    kv,
    qg,
    kt,
    prob,
    dprob,
    top,
    total,
    dtotal,
    bias,
    stat,
    dstat,
    factor,
    delta,
    term,
    term_in,
    dq_out,
    dq_in,
    ids_ref,
    lists_ref,
    load_sem,
    kv_send,
    kv_recv,
    qg_send,
    qg_recv,
    stat_sem,
    dstat_sem,
    term_send,
    term_recv,
    dq_send,
    dq_recv,
):
    rows = k_ref.shape[0]
    width = k_ref.shape[1]
    piece = rows // 2
    tiles = 2 * heads
    half = heads * rows
    scale = width**-0.5
    scale2 = scale * LOG2E

    outer = lax.axis_index("outer")
    inner = lax.axis_index("inner")
    core = lax.rem(inner, 2)
    other = inner + 1 - 2 * core
    across = lax.rem(inner + 2, 4)
    up = lax.rem(outer + 1, outer_count)
    down = lax.rem(outer + outer_count - 1, outer_count)
    sibling = (outer, other)
    beside = (outer, across)

    def remote(src, dst, send, recv, device):
        return pltpu.make_async_remote_copy(
            src_ref=src, dst_ref=dst, send_sem=send, recv_sem=recv, device_id=device, device_id_type=MESH
        )

    loads_ids = [
        pltpu.make_async_copy(ids_hbm, ids_ref, load_sem.at[4]),
        pltpu.make_async_copy(lists_hbm, lists_ref, load_sem.at[5]),
    ]
    for c in loads_ids:
        c.start()
    loads_kv = [
        pltpu.make_async_copy(k_ref, kv.at[0, 0], load_sem.at[0]),
        pltpu.make_async_copy(v_ref, kv.at[1, 0], load_sem.at[1]),
    ]
    for c in loads_kv:
        c.start()
    loads_q = []
    for which, src in ((0, q_ref), (1, g_ref)):
        for h in range(heads):
            loads_q.append(
                pltpu.make_async_copy(
                    src.at[:, pl.ds(h * width, width)],
                    qg.at[which, pl.ds(h * rows, rows)],
                    load_sem.at[2 + which],
                )
            )
    for c in loads_q:
        c.start()

    barrier = pltpu.get_barrier_semaphore()
    for device in (sibling, beside, (down, inner), (down, across)):
        pl.semaphore_signal(barrier, inc=1, device_id=device, device_id_type=MESH)
    pl.semaphore_wait(barrier, 4)

    for c in loads_kv:
        c.wait()
    kv_copies = {}
    for which in range(2):
        for slot, device in ((2, (up, inner)), (3, (up, across)), (1, beside)):
            index = 2 * slot + which
            kv_copies[slot, which] = remote(
                kv.at[which, 0], kv.at[which, slot], kv_send.at[index], kv_recv.at[index], device
            )
    for slot in (2, 3, 1):
        kv_copies[slot, 0].start()
    for which, src in ((0, q_ref), (1, g_ref)):
        for h in range(heads):
            c = remote(
                src.at[:, pl.ds(h * width, width)],
                qg.at[which, pl.ds(half + h * rows, rows)],
                qg_send.at[which],
                qg_recv.at[which],
                sibling,
            )
            c.start()

    for c in loads_ids:
        c.wait()
    slot_index = lax.broadcasted_iota(jnp.int32, (8, 1), 0)
    ids = jnp.zeros((8, 1), jnp.int32)
    for slot, (group, device) in enumerate(
        ((outer, inner), (outer, across), (down, inner), (down, across))
    ):
        for a in range(2):
            ids = jnp.where(slot_index == 2 * slot + a, ids_ref[group * 8 + device * 2 + a], ids)
    for who, device in ((0, inner), (1, other)):
        parts = []
        for a in range(2):
            row = lists_ref[pl.ds(2 * device + a, 1), :]
            hit = jnp.max(jnp.where(row == ids, 1.0, 0.0), axis=1, keepdims=True)
            parts.append(jnp.broadcast_to((hit - 1.0) * (-FILL), (8, piece)))
        both = jnp.concatenate(parts, axis=1)
        for j in range(8):
            bias[who, j] = jnp.broadcast_to(both[j : j + 1], (8, rows))

    causal = lax.broadcasted_iota(jnp.int32, (piece, piece), 0) <= lax.broadcasted_iota(
        jnp.int32, (piece, piece), 1
    )

    def scores(slot, who):
        def head(h, _):
            t = who * heads + h
            lanes = pl.ds(pl.multiple_of(t * rows, rows), rows)
            s = dot_nt(kv[0, slot], qg[0, lanes, :])
            for a in range(2):
                sa = s[a * piece : (a + 1) * piece]
                if slot == 0 and who == 0:
                    cut = jnp.where(causal, sa[:, a * piece : (a + 1) * piece], FILL)
                    sa = jnp.concatenate(
                        [cut, sa[:, piece:]] if a == 0 else [sa[:, :piece], cut], axis=1
                    )
                s3 = sa.reshape(piece // 8, 8, rows)
                m = jnp.max(s3, axis=0)
                p = jnp.exp2((s3 - m[None]) * scale2)
                prob[pl.ds(slot * rows + a * piece, piece), lanes] = p.reshape(piece, rows).astype(BF16)
                top[t, 2 * slot + a] = m * scale2
                total[t, 2 * slot + a] = jnp.sum(p, axis=0)
            return 0

        lax.fori_loop(0, heads, head, 0, unroll=True)

    def dscores_part(slot, who):
        def head(h, _):
            t = who * heads + h
            lanes = pl.ds(pl.multiple_of(t * rows, rows), rows)
            g = dot_nt(kv[1, slot], qg[1, lanes, :])
            for a in range(2):
                ga = g[a * piece : (a + 1) * piece]
                place = pl.ds(slot * rows + a * piece, piece)
                p = prob[place, lanes].astype(F32).reshape(piece // 8, 8, rows)
                dprob[place, lanes] = ga.astype(BF16)
                dtotal[t, 2 * slot + a] = jnp.sum(p * ga.reshape(piece // 8, 8, rows), axis=0)
            return 0

        lax.fori_loop(0, heads, head, 0, unroll=True)

    def transposed_keys(slot):
        kt[:, pl.ds(slot * rows, rows)] = kv[0, slot].T

    def loaded(which):
        pltpu.make_async_copy(
            qg.at[which, pl.ds(half, half)], qg.at[which, pl.ds(0, half)], load_sem.at[2 + which]
        ).wait()

    qg_all = [
        remote(
            qg.at[which, pl.ds(0, half)],
            qg.at[which, pl.ds(half, half)],
            qg_send.at[which],
            qg_recv.at[which],
            sibling,
        )
        for which in range(2)
    ]

    transposed_keys(0)
    loaded(0)
    scores(0, 0)
    qg_all[0].wait_recv()
    scores(0, 1)
    for slot in (2, 3, 1):
        kv_copies[slot, 1].start()
    loaded(1)
    dscores_part(0, 0)
    qg_all[1].wait_recv()
    dscores_part(0, 1)
    kv_copies[1, 0].wait_recv()
    scores(1, 0)
    scores(1, 1)
    transposed_keys(1)
    kv_copies[2, 0].wait_recv()
    scores(2, 0)
    scores(2, 1)
    transposed_keys(2)
    kv_copies[3, 0].wait_recv()
    scores(3, 0)
    scores(3, 1)

    for who in range(2):

        def local(h, _, who=who):
            t = who * heads + h
            mj = top[t] + bias[who]
            m = jnp.max(jnp.max(mj, axis=0), axis=0, keepdims=True)
            w = jnp.exp2(mj - m[None])
            top[t] = w
            stat[0, 0, pl.ds(t, 1)] = m
            stat[0, 1, pl.ds(t, 1)] = jnp.sum(jnp.sum(w * total[t], axis=0), axis=0, keepdims=True)
            return 0

        lax.fori_loop(0, heads, local, 0, unroll=True)
    stat_copy = remote(stat.at[0], stat.at[1], stat_sem.at[0], stat_sem.at[1], sibling)
    stat_copy.start()

    transposed_keys(3)
    kv_copies[1, 1].wait_recv()
    dscores_part(1, 0)
    dscores_part(1, 1)
    kv_copies[2, 1].wait_recv()
    dscores_part(2, 0)
    dscores_part(2, 1)

    def swapped(x):
        return jnp.concatenate([x[heads:], x[:heads]], axis=0)

    stat_copy.wait()
    m_mine, m_theirs = stat[0, 0], swapped(stat[1, 0])
    m = jnp.maximum(m_mine, m_theirs)
    e_mine = jnp.exp2(m_mine - m)
    norm = stat[0, 1] * e_mine + swapped(stat[1, 1]) * jnp.exp2(m_theirs - m)
    factor[...] = e_mine * (1.0 / norm)

    term_copies = {}
    for slot, device in ((1, beside), (3, (down, across)), (2, (down, inner))):
        for which in range(2):
            index = 2 * (slot - 1) + which
            term_copies[slot, which] = remote(
                term.at[slot - 1, which],
                term_in.at[slot - 1, which],
                term_send.at[index],
                term_recv.at[index],
                device,
            )

    def value_gradient(slot):
        def tile(t, value_term):
            lanes = pl.ds(pl.multiple_of(t * rows, rows), rows)
            f = factor[pl.ds(t, 1)]
            weights = []
            for a in range(2):
                r = (top[t, 2 * slot + a] * f).astype(BF16)
                r = jnp.concatenate([r, r], axis=0)
                place = pl.ds(slot * rows + a * piece, piece)
                p = prob[place, lanes].reshape(piece // 16, 16, rows) * r[None]
                weights.append(p.reshape(piece, rows))
            p = jnp.concatenate(weights, axis=0)
            prob[pl.ds(slot * rows, rows), lanes] = p
            return value_term + dot_nn(p, qg[1, lanes, :])

        value_term = lax.fori_loop(0, tiles, tile, jnp.zeros((rows, width), F32), unroll=True)
        if slot == 0:
            return value_term
        term[slot - 1, 1] = value_term.astype(BF16)
        term_copies[slot, 1].start()

    value_gradient(1)
    kv_copies[3, 1].wait_recv()
    dscores_part(3, 0)
    dscores_part(3, 1)

    def dlocal(t, _):
        d = jnp.sum(jnp.sum(top[t] * dtotal[t], axis=0), axis=0, keepdims=True)
        dstat[0, pl.ds(t, 1)] = d * factor[pl.ds(t, 1)]
        return 0

    lax.fori_loop(0, tiles, dlocal, 0, unroll=True)
    dstat_copy = remote(dstat.at[0], dstat.at[1], dstat_sem.at[0], dstat_sem.at[1], sibling)
    dstat_copy.start()
    value_gradient(2)
    value_gradient(3)
    own_value = value_gradient(0)
    dstat_copy.wait()
    d = dstat[0] + swapped(dstat[1])
    for t in range(tiles):
        delta[:, pl.ds(t * rows, rows)] = jnp.broadcast_to(d[t : t + 1], (16, rows)).astype(BF16)

    def key_gradient(slot, who, key_term):
        def tile(h, key_term):
            t = who * heads + h
            lanes = pl.ds(pl.multiple_of(t * rows, rows), rows)
            place = pl.ds(slot * rows, rows)
            de = delta[:, lanes]
            ds = prob[place, lanes].reshape(rows // 16, 16, rows) * (
                dprob[place, lanes].reshape(rows // 16, 16, rows) - de[None]
            )
            ds = ds.reshape(rows, rows)
            dprob[place, lanes] = ds
            return key_term + dot_nn(ds, qg[0, lanes, :])

        return lax.fori_loop(0, heads, tile, key_term, unroll=True)

    def key_send(slot, key_term):
        term[slot - 1, 0] = (key_term * scale).astype(BF16)
        term_copies[slot, 0].start()

    def query_gradient(t):
        lanes = pl.ds(pl.multiple_of(t * rows, rows), rows)
        return dot_nn(kt[...], dprob[:, lanes]).T * scale

    zero = jnp.zeros((rows, width), F32)
    key_send(1, key_gradient(1, 0, key_gradient(1, 1, zero)))
    partial = {slot: key_gradient(slot, 1, zero) for slot in (2, 3, 0)}
    dq_copies = []
    for c in range(4):
        for h in (2 * c, 2 * c + 1):
            dq_out[:, h * width : (h + 1) * width] = query_gradient(heads + h).astype(BF16)
        lanes = pl.ds(2 * c * width, 2 * width)
        copy = remote(dq_out.at[:, lanes], dq_in.at[:, lanes], dq_send.at[c], dq_recv.at[c], sibling)
        copy.start()
        dq_copies.append(copy)
    for slot in (2, 3):
        key_send(slot, key_gradient(slot, 0, partial[slot]))
    own_key = key_gradient(0, 0, partial[0]) * scale
    dq_own = [query_gradient(h) for h in range(heads)]
    for c in range(4):
        dq_copies[c].wait()
        for h in (2 * c, 2 * c + 1):
            lanes = pl.ds(h * width, width)
            dq_ref[:, lanes] = (dq_own[h] + dq_in[:, lanes].astype(F32)).astype(BF16)

    for c in term_copies.values():
        c.wait()
    for which, own, out in ((0, own_key, dk_ref), (1, own_value, dv_ref)):
        others = term_in[0, which].astype(F32) + term_in[1, which].astype(F32)
        out[...] = (own + (others + term_in[2, which].astype(F32))).astype(BF16)
    for c in kv_copies.values():
        c.wait_send()
    for c in qg_all:
        c.wait_send()


def solution(mesh):
    outer_count = mesh.shape["outer"]

    def per_device(query_rows, key_rows, value_rows, out_grad, piece_ids, key_pieces):
        rows, width = key_rows.shape
        heads = query_rows.shape[1] // width
        tiles = 2 * heads
        lanes = tiles * rows
        vmem = pl.BlockSpec(memory_space=pltpu.VMEM)
        return pl.pallas_call(
            functools.partial(kernel, outer_count, heads),
            out_shape=[
                jax.ShapeDtypeStruct(query_rows.shape, BF16),
                jax.ShapeDtypeStruct(key_rows.shape, BF16),
                jax.ShapeDtypeStruct(key_rows.shape, BF16),
            ],
            in_specs=[pl.BlockSpec(memory_space=pltpu.HBM)] * 6,
            out_specs=[vmem] * 3,
            scratch_shapes=[
                pltpu.VMEM((2, 4, rows, width), BF16),
                pltpu.VMEM((2, lanes, width), BF16),
                pltpu.VMEM((width, 4 * rows), BF16),
                pltpu.VMEM((4 * rows, lanes), BF16),
                pltpu.VMEM((4 * rows, lanes), BF16),
                pltpu.VMEM((tiles, 8, 8, rows), F32),
                pltpu.VMEM((tiles, 8, 8, rows), F32),
                pltpu.VMEM((tiles, 8, 8, rows), F32),
                pltpu.VMEM((2, 8, 8, rows), F32),
                pltpu.VMEM((2, 2, tiles, rows), F32),
                pltpu.VMEM((2, tiles, rows), F32),
                pltpu.VMEM((tiles, rows), F32),
                pltpu.VMEM((16, lanes), BF16),
                pltpu.VMEM((3, 2, rows, width), BF16),
                pltpu.VMEM((3, 2, rows, width), BF16),
                pltpu.VMEM(query_rows.shape, BF16),
                pltpu.VMEM(query_rows.shape, BF16),
                pltpu.SMEM(piece_ids.shape, jnp.int32),
                pltpu.VMEM(key_pieces.shape, jnp.int32),
                pltpu.SemaphoreType.DMA((6,)),
                pltpu.SemaphoreType.DMA((8,)),
                pltpu.SemaphoreType.DMA((8,)),
                pltpu.SemaphoreType.DMA((2,)),
                pltpu.SemaphoreType.DMA((2,)),
                pltpu.SemaphoreType.DMA((2,)),
                pltpu.SemaphoreType.DMA((2,)),
                pltpu.SemaphoreType.DMA((6,)),
                pltpu.SemaphoreType.DMA((6,)),
                pltpu.SemaphoreType.DMA((4,)),
                pltpu.SemaphoreType.DMA((4,)),
            ],
            compiler_params=pltpu.CompilerParams(
                collective_id=0, has_side_effects=True, vmem_limit_bytes=64 * 1024 * 1024
            ),
            name="attention_backward",
        )(query_rows, out_grad, key_rows, value_rows, piece_ids, key_pieces)

    return jax.shard_map(
        per_device,
        mesh=mesh,
        in_specs=(
            P(("outer", "inner"), None),
            P(("outer", "inner"), None),
            P(("outer", "inner"), None),
            P(("outer", "inner"), None),
            P(),
            P("outer", None),
        ),
        out_specs=(
            P(("outer", "inner"), None),
            P(("outer", "inner"), None),
            P(("outer", "inner"), None),
        ),
        check_vma=False,
    )
```

```python
import functools

import jax
import jax.numpy as jnp
from jax import lax
from jax.experimental import pallas as pl
from jax.experimental.pallas import tpu as pltpu
from jax.sharding import PartitionSpec as P

MESH = pl.DeviceIdType.MESH
F32 = jnp.float32
BF16 = jnp.bfloat16
LOG2E = 1.4426950408889634
FILL = -1e30


def dot_nt(a, b):
    return lax.dot_general(a, b, (((1,), (1,)), ((), ())), preferred_element_type=F32)


def dot_nn(a, b):
    return lax.dot_general(a, b, (((1,), (0,)), ((), ())), preferred_element_type=F32)


def kernel(
    outer_count,
    heads,
    q_ref,
    g_ref,
    k_ref,
    v_ref,
    ids_hbm,
    lists_hbm,
    dq_ref,
    dk_ref,
    dv_ref,
    kv,
    qg,
    kt,
    prob,
    dprob,
    top,
    total,
    dtotal,
    bias,
    stat,
    dstat,
    factor,
    delta,
    term,
    term_in,
    dq_out,
    dq_in,
    ids_ref,
    lists_ref,
    load_sem,
    kv_send,
    kv_recv,
    qg_send,
    qg_recv,
    stat_sem,
    dstat_sem,
    term_send,
    term_recv,
    dq_send,
    dq_recv,
):
    rows = k_ref.shape[0]
    width = k_ref.shape[1]
    piece = rows // 2
    tiles = 2 * heads
    half = heads * rows
    scale = width**-0.5
    scale2 = scale * LOG2E

    outer = lax.axis_index("outer")
    inner = lax.axis_index("inner")
    core = lax.rem(inner, 2)
    other = inner + 1 - 2 * core
    across = lax.rem(inner + 2, 4)
    up = lax.rem(outer + 1, outer_count)
    down = lax.rem(outer + outer_count - 1, outer_count)
    sibling = (outer, other)
    beside = (outer, across)

    def remote(src, dst, send, recv, device):
        return pltpu.make_async_remote_copy(
            src_ref=src, dst_ref=dst, send_sem=send, recv_sem=recv, device_id=device, device_id_type=MESH
        )

    loads_ids = [
        pltpu.make_async_copy(ids_hbm, ids_ref, load_sem.at[4]),
        pltpu.make_async_copy(lists_hbm, lists_ref, load_sem.at[5]),
    ]
    for c in loads_ids:
        c.start()
    loads_kv = [
        pltpu.make_async_copy(k_ref, kv.at[0, 0], load_sem.at[0]),
        pltpu.make_async_copy(v_ref, kv.at[1, 0], load_sem.at[1]),
    ]
    for c in loads_kv:
        c.start()
    loads_q = []
    for which, src in ((0, q_ref), (1, g_ref)):
        for h in range(heads):
            loads_q.append(
                pltpu.make_async_copy(
                    src.at[:, pl.ds(h * width, width)],
                    qg.at[which, pl.ds(h * rows, rows)],
                    load_sem.at[2 + which],
                )
            )
    for c in loads_q:
        c.start()

    barrier = pltpu.get_barrier_semaphore()
    for device in (sibling, beside, (down, inner), (down, across)):
        pl.semaphore_signal(barrier, inc=1, device_id=device, device_id_type=MESH)
    pl.semaphore_wait(barrier, 4)

    for c in loads_kv:
        c.wait()
    kv_copies = {}
    for which in range(2):
        for slot, device in ((2, (up, inner)), (3, (up, across)), (1, beside)):
            index = 2 * slot + which
            kv_copies[slot, which] = remote(
                kv.at[which, 0], kv.at[which, slot], kv_send.at[index], kv_recv.at[index], device
            )
    for slot in (2, 3, 1):
        kv_copies[slot, 0].start()
    for which, src in ((0, q_ref), (1, g_ref)):
        for h in range(heads):
            c = remote(
                src.at[:, pl.ds(h * width, width)],
                qg.at[which, pl.ds(half + h * rows, rows)],
                qg_send.at[which],
                qg_recv.at[which],
                sibling,
            )
            c.start()

    for c in loads_ids:
        c.wait()
    slot_index = lax.broadcasted_iota(jnp.int32, (8, 1), 0)
    ids = jnp.zeros((8, 1), jnp.int32)
    for slot, (group, device) in enumerate(
        ((outer, inner), (outer, across), (down, inner), (down, across))
    ):
        for a in range(2):
            ids = jnp.where(slot_index == 2 * slot + a, ids_ref[group * 8 + device * 2 + a], ids)
    for who, device in ((0, inner), (1, other)):
        parts = []
        for a in range(2):
            row = lists_ref[pl.ds(2 * device + a, 1), :]
            hit = jnp.max(jnp.where(row == ids, 1.0, 0.0), axis=1, keepdims=True)
            parts.append(jnp.broadcast_to((hit - 1.0) * (-FILL), (8, piece)))
        both = jnp.concatenate(parts, axis=1)
        for j in range(8):
            bias[who, j] = jnp.broadcast_to(both[j : j + 1], (8, rows))

    causal = lax.broadcasted_iota(jnp.int32, (piece, piece), 0) <= lax.broadcasted_iota(
        jnp.int32, (piece, piece), 1
    )

    def scores(slot, who):
        def head(h, _):
            t = who * heads + h
            lanes = pl.ds(pl.multiple_of(t * rows, rows), rows)
            s = dot_nt(kv[0, slot], qg[0, lanes, :])
            for a in range(2):
                sa = s[a * piece : (a + 1) * piece]
                if slot == 0 and who == 0:
                    cut = jnp.where(causal, sa[:, a * piece : (a + 1) * piece], FILL)
                    sa = jnp.concatenate(
                        [cut, sa[:, piece:]] if a == 0 else [sa[:, :piece], cut], axis=1
                    )
                s3 = sa.reshape(piece // 8, 8, rows)
                m = jnp.max(s3, axis=0)
                p = jnp.exp2((s3 - m[None]) * scale2)
                prob[pl.ds(slot * rows + a * piece, piece), lanes] = p.reshape(piece, rows).astype(BF16)
                top[t, 2 * slot + a] = m * scale2
                total[t, 2 * slot + a] = jnp.sum(p, axis=0)
            return 0

        lax.fori_loop(0, heads, head, 0, unroll=True)

    def dscores_part(slot, who):
        def head(h, _):
            t = who * heads + h
            lanes = pl.ds(pl.multiple_of(t * rows, rows), rows)
            g = dot_nt(kv[1, slot], qg[1, lanes, :])
            for a in range(2):
                ga = g[a * piece : (a + 1) * piece]
                place = pl.ds(slot * rows + a * piece, piece)
                p = prob[place, lanes].astype(F32).reshape(piece // 8, 8, rows)
                dprob[place, lanes] = ga.astype(BF16)
                dtotal[t, 2 * slot + a] = jnp.sum(p * ga.reshape(piece // 8, 8, rows), axis=0)
            return 0

        lax.fori_loop(0, heads, head, 0, unroll=True)

    def transposed_keys(slot):
        kt[:, pl.ds(slot * rows, rows)] = kv[0, slot].T

    def loaded(which):
        pltpu.make_async_copy(
            qg.at[which, pl.ds(half, half)], qg.at[which, pl.ds(0, half)], load_sem.at[2 + which]
        ).wait()

    qg_all = [
        remote(
            qg.at[which, pl.ds(0, half)],
            qg.at[which, pl.ds(half, half)],
            qg_send.at[which],
            qg_recv.at[which],
            sibling,
        )
        for which in range(2)
    ]

    transposed_keys(0)
    loaded(0)
    scores(0, 0)
    qg_all[0].wait_recv()
    scores(0, 1)
    for slot in (2, 3, 1):
        kv_copies[slot, 1].start()
    loaded(1)
    dscores_part(0, 0)
    qg_all[1].wait_recv()
    dscores_part(0, 1)
    kv_copies[1, 0].wait_recv()
    scores(1, 0)
    scores(1, 1)
    transposed_keys(1)
    kv_copies[2, 0].wait_recv()
    scores(2, 0)
    scores(2, 1)
    transposed_keys(2)
    kv_copies[3, 0].wait_recv()
    scores(3, 0)
    scores(3, 1)

    for who in range(2):

        def local(h, _, who=who):
            t = who * heads + h
            mj = top[t] + bias[who]
            m = jnp.max(jnp.max(mj, axis=0), axis=0, keepdims=True)
            w = jnp.exp2(mj - m[None])
            top[t] = w
            stat[0, 0, pl.ds(t, 1)] = m
            stat[0, 1, pl.ds(t, 1)] = jnp.sum(jnp.sum(w * total[t], axis=0), axis=0, keepdims=True)
            return 0

        lax.fori_loop(0, heads, local, 0, unroll=True)
    stat_copy = remote(stat.at[0], stat.at[1], stat_sem.at[0], stat_sem.at[1], sibling)
    stat_copy.start()

    transposed_keys(3)
    kv_copies[1, 1].wait_recv()
    dscores_part(1, 0)
    dscores_part(1, 1)
    kv_copies[2, 1].wait_recv()
    dscores_part(2, 0)
    dscores_part(2, 1)

    def swapped(x):
        return jnp.concatenate([x[heads:], x[:heads]], axis=0)

    stat_copy.wait()
    m_mine, m_theirs = stat[0, 0], swapped(stat[1, 0])
    m = jnp.maximum(m_mine, m_theirs)
    e_mine = jnp.exp2(m_mine - m)
    norm = stat[0, 1] * e_mine + swapped(stat[1, 1]) * jnp.exp2(m_theirs - m)
    factor[...] = e_mine * (1.0 / norm)

    term_copies = {}
    for slot, device in ((1, beside), (3, (down, across)), (2, (down, inner))):
        for which in range(2):
            index = 2 * (slot - 1) + which
            term_copies[slot, which] = remote(
                term.at[slot - 1, which],
                term_in.at[slot - 1, which],
                term_send.at[index],
                term_recv.at[index],
                device,
            )

    def value_gradient(slot):
        def tile(t, value_term):
            lanes = pl.ds(pl.multiple_of(t * rows, rows), rows)
            f = factor[pl.ds(t, 1)]
            weights = []
            for a in range(2):
                r = (top[t, 2 * slot + a] * f).astype(BF16)
                r = jnp.concatenate([r, r], axis=0)
                place = pl.ds(slot * rows + a * piece, piece)
                p = prob[place, lanes].reshape(piece // 16, 16, rows) * r[None]
                weights.append(p.reshape(piece, rows))
            p = jnp.concatenate(weights, axis=0)
            prob[pl.ds(slot * rows, rows), lanes] = p
            return value_term + dot_nn(p, qg[1, lanes, :])

        value_term = lax.fori_loop(0, tiles, tile, jnp.zeros((rows, width), F32), unroll=True)
        if slot == 0:
            return value_term
        term[slot - 1, 1] = value_term.astype(BF16)
        term_copies[slot, 1].start()

    value_gradient(1)
    kv_copies[3, 1].wait_recv()
    dscores_part(3, 0)
    dscores_part(3, 1)

    def dlocal(t, _):
        d = jnp.sum(jnp.sum(top[t] * dtotal[t], axis=0), axis=0, keepdims=True)
        dstat[0, pl.ds(t, 1)] = d * factor[pl.ds(t, 1)]
        return 0

    lax.fori_loop(0, tiles, dlocal, 0, unroll=True)
    dstat_copy = remote(dstat.at[0], dstat.at[1], dstat_sem.at[0], dstat_sem.at[1], sibling)
    dstat_copy.start()
    value_gradient(2)
    value_gradient(3)
    own_value = value_gradient(0)
    dstat_copy.wait()
    d = dstat[0] + swapped(dstat[1])
    for t in range(tiles):
        delta[:, pl.ds(t * rows, rows)] = jnp.broadcast_to(d[t : t + 1], (16, rows)).astype(BF16)

    def key_gradient(slot, who, key_term):
        def tile(h, key_term):
            t = who * heads + h
            lanes = pl.ds(pl.multiple_of(t * rows, rows), rows)
            place = pl.ds(slot * rows, rows)
            de = delta[:, lanes]
            ds = prob[place, lanes].reshape(rows // 16, 16, rows) * (
                dprob[place, lanes].reshape(rows // 16, 16, rows) - de[None]
            )
            ds = ds.reshape(rows, rows)
            dprob[place, lanes] = ds
            return key_term + dot_nn(ds, qg[0, lanes, :])

        return lax.fori_loop(0, heads, tile, key_term, unroll=True)

    def key_send(slot, key_term):
        term[slot - 1, 0] = (key_term * scale).astype(BF16)
        term_copies[slot, 0].start()

    def query_gradient(t):
        lanes = pl.ds(pl.multiple_of(t * rows, rows), rows)
        return dot_nn(kt[...], dprob[:, lanes]).T * scale

    zero = jnp.zeros((rows, width), F32)
    key_send(1, key_gradient(1, 0, key_gradient(1, 1, zero)))
    partial = {slot: key_gradient(slot, 1, zero) for slot in (2, 3, 0)}
    dq_copies = []
    for c in range(4):
        for h in (2 * c, 2 * c + 1):
            dq_out[:, h * width : (h + 1) * width] = query_gradient(heads + h).astype(BF16)
        lanes = pl.ds(2 * c * width, 2 * width)
        copy = remote(dq_out.at[:, lanes], dq_in.at[:, lanes], dq_send.at[c], dq_recv.at[c], sibling)
        copy.start()
        dq_copies.append(copy)
    for slot in (2, 3):
        key_send(slot, key_gradient(slot, 0, partial[slot]))
    own_key = key_gradient(0, 0, partial[0]) * scale
    dq_own = [query_gradient(h) for h in range(heads)]
    for c in range(4):
        dq_copies[c].wait()
        for h in (2 * c, 2 * c + 1):
            lanes = pl.ds(h * width, width)
            dq_ref[:, lanes] = (dq_own[h] + dq_in[:, lanes].astype(F32)).astype(BF16)

    for c in term_copies.values():
        c.wait()
    for which, own, out in ((0, own_key, dk_ref), (1, own_value, dv_ref)):
        others = term_in[0, which].astype(F32) + term_in[1, which].astype(F32)
        out[...] = (own + (others + term_in[2, which].astype(F32))).astype(BF16)
    for c in kv_copies.values():
        c.wait_send()
    for c in qg_all:
        c.wait_send()


def solution(mesh):
    outer_count = mesh.shape["outer"]

    def per_device(query_rows, key_rows, value_rows, out_grad, piece_ids, key_pieces):
        rows, width = key_rows.shape
        heads = query_rows.shape[1] // width
        tiles = 2 * heads
        lanes = tiles * rows
        vmem = pl.BlockSpec(memory_space=pltpu.VMEM)
        return pl.pallas_call(
            functools.partial(kernel, outer_count, heads),
            out_shape=[
                jax.ShapeDtypeStruct(query_rows.shape, BF16),
                jax.ShapeDtypeStruct(key_rows.shape, BF16),
                jax.ShapeDtypeStruct(key_rows.shape, BF16),
            ],
            in_specs=[pl.BlockSpec(memory_space=pltpu.HBM)] * 6,
            out_specs=[vmem] * 3,
            scratch_shapes=[
                pltpu.VMEM((2, 4, rows, width), BF16),
                pltpu.VMEM((2, lanes, width), BF16),
                pltpu.VMEM((width, 4 * rows), BF16),
                pltpu.VMEM((4 * rows, lanes), BF16),
                pltpu.VMEM((4 * rows, lanes), BF16),
                pltpu.VMEM((tiles, 8, 8, rows), F32),
                pltpu.VMEM((tiles, 8, 8, rows), F32),
                pltpu.VMEM((tiles, 8, 8, rows), F32),
                pltpu.VMEM((2, 8, 8, rows), F32),
                pltpu.VMEM((2, 2, tiles, rows), F32),
                pltpu.VMEM((2, tiles, rows), F32),
                pltpu.VMEM((tiles, rows), F32),
                pltpu.VMEM((16, lanes), BF16),
                pltpu.VMEM((3, 2, rows, width), BF16),
                pltpu.VMEM((3, 2, rows, width), BF16),
                pltpu.VMEM(query_rows.shape, BF16),
                pltpu.VMEM(query_rows.shape, BF16),
                pltpu.SMEM(piece_ids.shape, jnp.int32),
                pltpu.VMEM(key_pieces.shape, jnp.int32),
                pltpu.SemaphoreType.DMA((6,)),
                pltpu.SemaphoreType.DMA((8,)),
                pltpu.SemaphoreType.DMA((8,)),
                pltpu.SemaphoreType.DMA((2,)),
                pltpu.SemaphoreType.DMA((2,)),
                pltpu.SemaphoreType.DMA((2,)),
                pltpu.SemaphoreType.DMA((2,)),
                pltpu.SemaphoreType.DMA((6,)),
                pltpu.SemaphoreType.DMA((6,)),
                pltpu.SemaphoreType.DMA((4,)),
                pltpu.SemaphoreType.DMA((4,)),
            ],
            compiler_params=pltpu.CompilerParams(
                collective_id=0, has_side_effects=True, vmem_limit_bytes=48 * 1024 * 1024
            ),
            name="attention_backward",
        )(*[pltpu.with_memory_space_constraint(x, pltpu.HBM) for x in (query_rows, out_grad, key_rows, value_rows, piece_ids, key_pieces)])

    return jax.shard_map(
        per_device,
        mesh=mesh,
        in_specs=(
            P(("outer", "inner"), None),
            P(("outer", "inner"), None),
            P(("outer", "inner"), None),
            P(("outer", "inner"), None),
            P(),
            P("outer", None),
        ),
        out_specs=(
            P(("outer", "inner"), None),
            P(("outer", "inner"), None),
            P(("outer", "inner"), None),
        ),
        check_vma=False,
    )
```
